32 devices in a mesh: groups: 2 (over y), tensor: 16 (over z, x, core).
Axes of the slice: x: 2, y: 2, z: 4, core: 2. Of those that a mesh axis runs over, the one named last changes fastest.
Arguments:
- inputs: bfloat16 [256, 8192], P(('groups', 'tensor')), parts along dimension 0, may hold values from -6 to 6
- tangent: bfloat16 [256, 8192], P(('groups', 'tensor')), parts along dimension 0, may hold values from -6 to 6
- token_ids: int32 [256], P('groups'), parts along dimension 0, may hold values from 0 to 64127
- gate_weight: bfloat16 [8192, 28672], P(None, 'tensor'), may hold values from -0.0625 to 0.0625
- up_weight: bfloat16 [8192, 28672], P(None, 'tensor'), may hold values from -0.0625 to 0.0625
- down_weight: bfloat16 [28672, 8192], P('tensor'), may hold values from -0.046875 to 0.046875
- sketch: bfloat16 [8192, 1024], P('tensor'), may hold values from -0.09375 to 0.09375
- teacher_precision: bfloat16 [64128, 1024], P(None, 'tensor'), may hold values from 0.099609375 to 10
Outputs:
- curvature: float32 [256, 8192], P(('groups', 'tensor')), parts along dimension 0
The draws below stay inside these ranges and needn't reach their ends.
There are 2 independent parts, one for each index of `groups`. The reference program is written for one: setup_inputs(seed, part) draws one part's arguments, and reference() takes and returns one part's arrays. A program takes and returns all parts, laid end to end along the dimension named above; an argument that names none is the same for every part. Nothing has to cross between parts.
All inputs are finite; a program needn't handle non-finite values.
Results may differ from the reference program's by a relative error of at most 0.006.
Values may be sent and summed in bfloat16 or wider, within the bound.
A program may use at most 256 MiB of HBM per device.

```python
import math
import jax
import jax.numpy as jnp
import numpy as np
from jax import lax

D = 8192
FF = 28672
R = 1024
VOCAB = 64128
ROWS = 128


def place_ends(result, own_key, low, high):
    index_at = [jax.random.randint(jax.random.fold_in(own_key, axis), (), 0, length) for axis, length in enumerate(result.shape)]
    main_axis = result.shape.index(max(result.shape))
    beside = index_at[:main_axis] + [(index_at[main_axis] + 1) % result.shape[main_axis]] + index_at[main_axis + 1:]
    return result.at[tuple(index_at)].set(low).at[tuple(beside)].set(high)


def strengthened(values, key, source, target, shards_of, factor):
    def block_of(axis_at):
        return (jnp.arange(values.shape[axis_at]) // (values.shape[axis_at] // shards_of)).reshape((-1,) + (1,) * (values.ndim - 1 - axis_at))

    near = jax.random.permutation(key, shards_of)[block_of(target)]
    far = (block_of(target) + shards_of // 2) % shards_of
    return jnp.where((block_of(source) == near) | (block_of(source) == far), factor * values, values)


def block_levels(key, dims, shards, low, largest):
    def one(position, parts):
        heights = jax.random.uniform(jax.random.fold_in(jax.random.fold_in(key, 6), position), (parts,), jnp.float32, low / len(shards), largest / len(shards))
        return jnp.repeat(jnp.exp(heights), dims[position] // parts).reshape((-1,) + (1,) * (len(dims) - position - 1))

    level = one(*shards[0])
    for cut in shards[1:]:
        level = level * one(*cut)
    return level


def rank_table(count, lean):
    weights = [(1 << 20) // math.isqrt(standing ** lean) + 1 for standing in range(1, count + 1)]
    spread = 1 + sum(weights) // (1 << 30)
    return np.cumsum(np.array([max(1, weight // spread) for weight in weights]))


def ranked(stream_key, dims, number_of, skew):
    table = rank_table(number_of, skew)
    ticket = jax.random.randint(jax.random.fold_in(stream_key, 1), dims, 0, int(table[number_of - 1]))
    standing = jnp.searchsorted(jnp.asarray(table, jnp.int32), ticket, side="right")
    return jax.random.permutation(jax.random.fold_in(stream_key, 2), number_of)[standing].astype(jnp.int32)


def gaussian(key, shape, deviation, bound, pieces=(), dtype=jnp.bfloat16):
    result = deviation * jax.random.normal(key, shape, jnp.float32)
    if pieces:
        result = result * block_levels(key, shape, pieces, -0.22, 0.18)
    return jnp.clip(result, -bound, bound).astype(dtype)


def gaussian_with(rng, extent, scale, bound, pieces, heavy, kind=jnp.bfloat16):
    values = scale * jax.random.normal(rng, extent, jnp.float32)
    if pieces:
        values = values * block_levels(rng, extent, pieces, -0.22, 0.18)
    return jnp.clip(strengthened(values, jax.random.fold_in(rng, 3), *heavy), -bound, bound).astype(kind)


def setup_inputs(seed: int = 0, part: int = 0) -> dict:
    arg_keys = jax.random.split(jax.random.key(seed), 9)
    part_keys = jax.random.split(jax.random.fold_in(arg_keys[8], part), 9)
    inputs = gaussian(part_keys[0], (ROWS, D), 1.0, 6.0, ((0, 16),))
    tangent = gaussian(part_keys[1], (ROWS, D), 1.0, 6.0, ((0, 16),))
    token_ids = place_ends(ranked(part_keys[2], (ROWS,), VOCAB, 2), jax.random.fold_in(part_keys[2], 3), 0, VOCAB - 1).astype(jnp.int32)
    gate_weight = gaussian(arg_keys[3], (D, FF), D ** -0.5, 0.0625, ((1, 16),))
    up_weight = gaussian(arg_keys[4], (D, FF), D ** -0.5, 0.0625, ((1, 16),))
    down_weight = gaussian_with(arg_keys[5], (FF, D), FF ** -0.5, 0.046875, ((0, 16),), (0, 1, 16, 2.0))
    sketch = gaussian_with(arg_keys[6], (D, R), D ** -0.5, 0.09375, ((0, 16),), (0, 1, 16, 2.0))
    teacher_precision = jnp.clip(jnp.exp(math.log(10.0) - 4.609084 * jax.random.uniform(arg_keys[7], (VOCAB, R), jnp.float32) ** block_levels(arg_keys[7], (VOCAB, R), ((1, 16),), -0.2, 0.2)), 0.099609375, 10.0).astype(jnp.bfloat16)
    return {"inputs": inputs, "tangent": tangent, "token_ids": token_ids, "gate_weight": gate_weight, "up_weight": up_weight, "down_weight": down_weight, "sketch": sketch, "teacher_precision": teacher_precision}


def reference(inputs, tangent, token_ids, gate_weight, up_weight, down_weight, sketch, teacher_precision):
    pre_gate = jnp.dot(inputs, gate_weight, preferred_element_type=jnp.float32)
    pre_up = jnp.dot(inputs, up_weight, preferred_element_type=jnp.float32)
    tan_gate = jnp.dot(tangent, gate_weight, preferred_element_type=jnp.float32)
    tan_up = jnp.dot(tangent, up_weight, preferred_element_type=jnp.float32)
    sig = jax.nn.sigmoid(pre_gate)
    act = pre_gate * sig
    slope = sig * (1.0 + pre_gate * (1.0 - sig))
    tan_hidden = (slope * tan_gate * pre_up + act * tan_up).astype(jnp.bfloat16)
    tan_out = tangent.astype(jnp.float32) + jnp.dot(tan_hidden, down_weight, preferred_element_type=jnp.float32)
    tan_sketch = jnp.dot(tan_out, sketch.astype(jnp.float32), precision=lax.Precision.HIGHEST)
    rows_prec = teacher_precision[token_ids].astype(jnp.float32)
    weighted = (rows_prec * tan_sketch).astype(jnp.bfloat16)
    cot = jnp.dot(weighted, sketch.T, preferred_element_type=jnp.float32)
    back_hidden = jnp.dot(cot.astype(jnp.bfloat16), down_weight.T, preferred_element_type=jnp.float32)
    back_gate = (back_hidden * pre_up * slope).astype(jnp.bfloat16)
    back_up = (back_hidden * act).astype(jnp.bfloat16)
    curvature = cot + jnp.dot(back_gate, gate_weight.T, preferred_element_type=jnp.float32)
    curvature = curvature + jnp.dot(back_up, up_weight.T, preferred_element_type=jnp.float32)
    return curvature
```

```python
import functools

import jax
import jax.numpy as jnp
from jax import lax
from jax.experimental import pallas as pl
from jax.experimental.pallas import tpu as pltpu
from jax.sharding import PartitionSpec as P

F32 = jnp.float32
BF16 = jnp.bfloat16
NZ, NX, NC = 4, 2, 2
MESH = pl.DeviceIdType.MESH
VMEM = pltpu.VMEM
DMA = pltpu.SemaphoreType.DMA
LIMIT = 62 << 20


def place():
    me = lax.axis_index("tensor")
    return me, me // 4, (me // 2) % 2, me % 2


def index_of(z, x, c):
    return (z % NZ) * 4 + x * 2 + c


def greet(z, x, c):
    barrier = pltpu.get_barrier_semaphore()
    others = [index_of(z + k, x, c) for k in (1, 2, 3)]
    others += [index_of(z, 1 - x, c), index_of(z, x, 1 - c)]
    for other in others:
        pl.semaphore_signal(barrier, inc=1, device_id={"tensor": other}, device_id_type=MESH)
    pl.semaphore_wait(barrier, 5)


def remote(src, dst, send, recv, other):
    return pltpu.make_async_remote_copy(
        src_ref=src,
        dst_ref=dst,
        send_sem=send,
        recv_sem=recv,
        device_id={"tensor": other},
        device_id_type=MESH,
    )


def span(start, size):
    return pl.ds(pl.multiple_of(start, size), size)


def loop(lo, hi, body):
    def step(i, carry):
        body(i)
        return carry

    lax.fori_loop(lo, hi, step, 0)


def nt(a, b):
    return lax.dot_general(a, b, (((1,), (1,)), ((), ())), preferred_element_type=F32)


def nn(a, b):
    return jnp.dot(a, b, preferred_element_type=F32)


def forward_kernel(
    nf, fc, slots, feat,
    xv_ref, gate_ref, up_ref, th_ref, cg_ref, ca_ref, vc_ref,
    xg, wg, wu, acc_g, acc_u, wsem, zs, zr, xs, xr, cs, cr,
):
    me, z, x, c = place()
    hidden = th_ref.shape[1]

    def weights(f):
        slot = lax.rem(f, slots)
        rows = span(f * fc, fc)
        return (
            pltpu.make_async_copy(gate_ref.at[rows], wg.at[slot], wsem.at[0, slot]),
            pltpu.make_async_copy(up_ref.at[rows], wu.at[slot], wsem.at[1, slot]),
        )

    def fetch(f):
        for copy in weights(f):
            copy.start()

    loop(0, slots, fetch)
    slot_me = (c * NX + x) * NZ + z
    mine = span(slot_me * 16, 16)
    xg[mine, :] = xv_ref[...]
    greet(z, x, c)

    def send_z(f, k):
        cols = span(f * fc, fc)
        return remote(
            xv_ref.at[:, cols], xg.at[mine, cols], zs.at[f, k - 1], zr.at[f, k - 1],
            index_of(z + k, x, c),
        )

    def send_x(f):
        part = xg.at[span((c * NX + x) * 64, 64), span(f * fc, fc)]
        return remote(part, part, xs.at[f], xr.at[f], index_of(z, 1 - x, c))

    def send_c(f):
        part = xg.at[span(c * 128, 128), span(f * fc, fc)]
        return remote(part, part, cs.at[f], cr.at[f], index_of(z, x, 1 - c))

    def first(f):
        for k in (1, 2, 3):
            send_z(f, k).start()

    loop(0, nf, first)
    acc_g[...] = jnp.zeros_like(acc_g)
    acc_u[...] = jnp.zeros_like(acc_u)

    def step(s):
        @pl.when(s < nf)
        def _():
            for k in (1, 2, 3):
                send_z(s, k).wait_recv()
            send_x(s).start()

        @pl.when((s >= 1) & (s <= nf))
        def _():
            send_x(s - 1).wait_recv()
            send_c(s - 1).start()

        @pl.when(s >= 2)
        def _():
            f = s - 2
            send_c(f).wait_recv()
            for copy in weights(f):
                copy.wait()
            slot = lax.rem(f, slots)
            block = xg[:, span(f * fc, fc)]
            acc_g[...] += nn(block, wg[slot])
            acc_u[...] += nn(block, wu[slot])

            @pl.when(f + slots < nf)
            def _():
                fetch(f + slots)

    loop(0, nf + 2, step)

    tile = 256

    def finish(t):
        cols = span(t * tile, tile)
        both_g = acc_g[:, cols].reshape(16, 2, 8, tile)
        both_u = acc_u[:, cols].reshape(16, 2, 8, tile)
        pre_gate, tan_gate = both_g[:, 0].reshape(128, tile), both_g[:, 1].reshape(128, tile)
        pre_up, tan_up = both_u[:, 0].reshape(128, tile), both_u[:, 1].reshape(128, tile)
        sig = jax.nn.sigmoid(pre_gate)
        act = pre_gate * sig
        slope = sig * (1.0 + pre_gate * (1.0 - sig))
        coef = pre_up * slope
        th_ref[:, cols] = (slope * tan_gate * pre_up + act * tan_up).astype(BF16)
        cg_ref[:, cols] = coef
        ca_ref[:, cols] = act

    loop(0, hidden // tile, finish)
    own = xg[:, span(me * feat, feat)].astype(F32).reshape(16, 2, 8, feat)
    vc_ref[...] = own[:, 1].reshape(128, feat)

    def drain(f):
        for k in (1, 2, 3):
            send_z(f, k).wait_send()
        send_x(f).wait_send()
        send_c(f).wait_send()

    loop(0, nf, drain)


def middle_kernel(
    th_ref, cg_ref, ca_ref, vc_ref, sk_ref, prec_ref, down_ref,
    bg_ref, bu_ref, cot_ref,
    dn, pbuf, rb, xsb, xrb, zsb, zrb, sk, rc, sxs, sxr, szs, szr, wga, cga, accb,
    dsem, s_send, s_recv, k_send, k_recv, w_send, w_recv, a_send, a_recv,
):
    me, z, x, c = place()
    x_peer, c_peer = index_of(z, 1 - x, c), index_of(z, x, 1 - c)
    width = pbuf.shape[2]
    feat = width // 4

    def weights(i):
        cols = span(((z + 1 + i) % NZ) * width, width)
        return pltpu.make_async_copy(down_ref.at[:, cols], dn.at[i], dsem.at[i])

    loop(0, NZ, lambda i: weights(i).start())
    greet(z, x, c)

    def cols_of(xx, cc):
        return span((xx * 2 + cc) * feat, feat)

    def rs_c(i, xx):
        return remote(
            pbuf.at[i, :, cols_of(xx, 1 - c)], rb.at[i, xx],
            s_send.at[i, xx], s_recv.at[i, xx], c_peer,
        )

    def rs_x(i):
        return remote(xsb.at[i], xrb.at[i], s_send.at[i, 2], s_recv.at[i, 2], x_peer)

    def rs_z(i):
        return remote(
            zsb.at[i], zrb.at[i], s_send.at[i, 3], s_recv.at[i, 3], index_of(z + 1 + i, x, c)
        )

    def step(s):
        @pl.when(s < NZ)
        def _():
            weights(s).wait()

            def tile(t):
                cols = span(t * feat, feat)
                pbuf[s, :, cols] = nn(th_ref[...], dn[s, :, cols])

            loop(0, 4, tile)
            rs_c(s, 0).start()
            rs_c(s, 1).start()

        @pl.when((s >= 1) & (s <= NZ))
        def _():
            i = s - 1
            rs_c(i, 0).wait_recv()
            rs_c(i, 1).wait_recv()
            xsb[i] = (pbuf[i, :, cols_of(1 - x, c)] + rb[i, 1 - x]).astype(BF16)
            rs_x(i).start()

        @pl.when((s >= 2) & (s <= NZ))
        def _():
            i = s - 2
            rs_x(i).wait_recv()
            total = pbuf[i, :, cols_of(x, c)] + rb[i, x] + xrb[i].astype(F32)
            zsb[i] = total.astype(BF16)
            rs_z(i).start()

    loop(0, NZ + 1, step)
    last = NZ - 1
    rs_x(last).wait_recv()
    total = pbuf[last, :, cols_of(x, c)] + rb[last, x] + xrb[last].astype(F32) + vc_ref[...]
    for i in range(NZ - 1):
        rs_z(i).wait_recv()
        total = total + zrb[i].astype(F32)

    high = total.astype(BF16)
    low = (total - high.astype(F32)).astype(BF16)
    part = nn(high, sk_ref[...]) + nn(low, sk_ref[...])
    sk[...] = part.T.reshape(sk.shape)
    copy_c = remote(sk.at[:, :, 1 - c], rc, k_send.at[0], k_recv.at[0], c_peer)
    copy_c.start()
    copy_c.wait_recv()
    sxs[...] = sk[:, 1 - x, c] + rc[:, 1 - x]
    copy_x = remote(sxs, sxr, k_send.at[1], k_recv.at[1], x_peer)
    copy_x.start()
    copy_x.wait_recv()
    szs[...] = sk[:, x, c] + rc[:, x] + sxr[...]
    copies = [
        remote(szs.at[(z + k) % NZ], szr.at[k - 1], k_send.at[1 + k], k_recv.at[1 + k],
               index_of(z + k, x, c))
        for k in (1, 2, 3)
    ]
    for copy in copies:
        copy.start()
    value = szs[z]
    for k, copy in enumerate(copies):
        copy.wait_recv()
        value = value + szr[k]
    for copy in copies + [copy_c, copy_x]:
        copy.wait_send()

    wga[z, x, c] = (prec_ref[...] * value).astype(BF16)
    mine = wga.at[z, x, c]
    copies = [
        remote(mine, mine, w_send.at[k - 1], w_recv.at[k - 1], index_of(z + k, x, c))
        for k in (1, 2, 3)
    ]
    for copy in copies:
        copy.start()
    for copy in copies:
        copy.wait_recv()
    copy_x = remote(wga.at[:, x, c], wga.at[:, x, c], w_send.at[3], w_recv.at[3], x_peer)
    copy_x.start()
    copy_x.wait_recv()
    copy_c = remote(wga.at[:, :, c], wga.at[:, :, c], w_send.at[4], w_recv.at[4], c_peer)
    copy_c.start()
    copy_c.wait_recv()
    for copy in copies + [copy_x, copy_c]:
        copy.wait_send()
    flat = wga[...].reshape(-1, 128).astype(F32).T.astype(BF16)
    cot = nt(flat, sk_ref[...])
    cot_ref[...] = cot

    cga[z, x, c] = cot.astype(BF16)

    def ag_z(k):
        part = cga.at[z, x, c]
        return remote(part, part, a_send.at[0, k], a_recv.at[0, k], index_of(z + k, x, c))

    def ag_x(k):
        part = cga.at[(z + NZ - k) % NZ, x, c]
        return remote(part, part, a_send.at[1, k], a_recv.at[1, k], x_peer)

    def ag_c(k, own):
        part = cga.at[(z + NZ - k) % NZ, x if own else 1 - x, c]
        row = 2 if own else 3
        return remote(part, part, a_send.at[row, k], a_recv.at[row, k], c_peer)

    def ag_c_other(k, own):
        return ag_c(k, own)

    def use(k, xx, cc):
        accb[...] += nt(cga[(z + NZ - k) % NZ, xx, cc], dn[3 - k, :, cols_of(xx, cc)])

    for k in (1, 2, 3):
        ag_z(k).start()
    accb[...] = jnp.zeros_like(accb)

    def own_column(k):
        @pl.when(k >= 1)
        def _():
            ag_z(k).wait_recv()

        ag_x(k).start()
        ag_c(k, True).start()
        use(k, x, c)

    loop(0, NZ, own_column)

    def other_column(k):
        ag_x(k).wait_recv()
        ag_c(k, False).start()
        use(k, 1 - x, c)

    loop(0, NZ, other_column)

    def sibling_own(k):
        ag_c_other(k, True).wait_recv()
        use(k, x, 1 - c)

    loop(0, NZ, sibling_own)

    def sibling_other(k):
        ag_c_other(k, False).wait_recv()
        use(k, 1 - x, 1 - c)

    loop(0, NZ, sibling_other)

    bg_ref[...] = (accb[...] * cg_ref[...]).astype(BF16)
    bu_ref[...] = (accb[...] * ca_ref[...]).astype(BF16)

    def drain(k):
        @pl.when(k >= 1)
        def _():
            ag_z(k).wait_send()
            rs_z(k - 1).wait_send()

        ag_x(k).wait_send()
        ag_c(k, True).wait_send()
        ag_c(k, False).wait_send()
        rs_c(k, 0).wait_send()
        rs_c(k, 1).wait_send()
        rs_x(k).wait_send()

    loop(0, NZ, drain)


def final_kernel(
    nf, fc, slots,
    bg_ref, bu_ref, cot_ref, gate_ref, up_ref, out_ref,
    wg, wu, pbuf, rb, xsb, xrb, tb, zsb, zrb, wsem, c_send, c_recv, x_send, x_recv, z_send, z_recv,
):
    me, z, x, c = place()
    x_peer, c_peer = index_of(z, 1 - x, c), index_of(z, x, 1 - c)
    feat = cot_ref.shape[1]
    half = fc // 2

    def weights(f):
        slot = lax.rem(f, slots)
        rows = span(f * fc, fc)
        return (
            pltpu.make_async_copy(gate_ref.at[rows], wg.at[slot], wsem.at[0, slot]),
            pltpu.make_async_copy(up_ref.at[rows], wu.at[slot], wsem.at[1, slot]),
        )

    def fetch(f):
        for copy in weights(f):
            copy.start()

    loop(0, slots, fetch)
    greet(z, x, c)

    def rs_c(f):
        return remote(
            pbuf.at[f, span((1 - c) * 64, 64)], rb.at[f], c_send.at[f], c_recv.at[f], c_peer
        )

    def rs_x(f):
        return remote(xsb.at[f], xrb.at[f], x_send.at[f], x_recv.at[f], x_peer)

    def rs_z(f, k):
        return remote(
            zsb.at[f, k - 1], zrb.at[f, k - 1], z_send.at[f, k - 1], z_recv.at[f, k - 1],
            index_of(z + k, x, c),
        )

    def step(s):
        @pl.when(s < nf)
        def _():
            for copy in weights(s):
                copy.wait()
            slot = lax.rem(s, slots)
            pbuf[s] = nt(bg_ref[...], wg[slot]) + nt(bu_ref[...], wu[slot])

            @pl.when(s == (me * feat) // fc)
            def _():
                cols = span(((me * feat) % fc) // feat * feat, feat)
                pbuf[s, :, cols] += cot_ref[...]

            rs_c(s).start()

            @pl.when(s + slots < nf)
            def _():
                fetch(s + slots)

        @pl.when((s >= 1) & (s <= nf))
        def _():
            f = s - 1
            rs_c(f).wait_recv()
            away = pbuf[f, span(c * 64 + (1 - x) * 32, 32)] + rb[f, span((1 - x) * 32, 32)]
            xsb[f] = away.astype(BF16)
            rs_x(f).start()

        @pl.when((s >= 2) & (s <= nf + 1))
        def _():
            f = s - 2
            rs_x(f).wait_recv()
            tb[...] = (
                pbuf[f, span(c * 64 + x * 32, 32)]
                + rb[f, span(x * 32, 32)]
                + xrb[f].astype(F32)
            )
            for k in (1, 2, 3):
                rows = tb[span(((z + k) % NZ) * 8, 8), :]
                folded = jnp.concatenate([rows[:, :half], rows[:, half:]], axis=0)
                zsb[f, k - 1] = folded.astype(BF16)
                rs_z(f, k).start()
            out_ref[:, span(f * fc, fc)] = tb[span(z * 8, 8), :]

        @pl.when(s >= 3)
        def _():
            f = s - 3
            total = out_ref[:, span(f * fc, fc)]
            for k in (1, 2, 3):
                rs_z(f, k).wait_recv()
                folded = zrb[f, k - 1].astype(F32)
                total = total + jnp.concatenate([folded[:8], folded[8:]], axis=1)
            out_ref[:, span(f * fc, fc)] = total

    loop(0, nf + 3, step)

    def drain(f):
        rs_c(f).wait_send()
        rs_x(f).wait_send()
        for k in (1, 2, 3):
            rs_z(f, k).wait_send()

    loop(0, nf, drain)


def rows_kernel(depth, ids_ref, table_ref, out_ref, buf, sem):
    count = out_ref.shape[1]

    def copy(t):
        slot = lax.rem(t, depth)
        block = pl.multiple_of(lax.shift_right_logical(ids_ref[t], 7) * 128, 128)
        return pltpu.make_async_copy(table_ref.at[:, pl.ds(block, 128)], buf.at[slot], sem.at[slot])

    loop(0, depth, lambda t: copy(t).start())
    lanes = lax.broadcasted_iota(jnp.int32, out_ref.shape, 1)

    def step(t, held):
        copy(t).wait()
        block = buf[lax.rem(t, depth)].astype(F32)
        shift = jnp.bitwise_and(t + 128 - jnp.bitwise_and(ids_ref[t], 127), 127)
        held = jnp.where(lanes == t, pltpu.roll(block, shift, axis=1), held)

        @pl.when(t + depth < count)
        def _():
            copy(t + depth).start()

        return held

    out_ref[...] = lax.fori_loop(0, count, step, jnp.zeros(out_ref.shape, F32))


ANY = pl.BlockSpec(memory_space=pl.ANY)
IN_VMEM = pl.BlockSpec(memory_space=pltpu.VMEM)


def params(collective_id):
    return pltpu.CompilerParams(
        collective_id=collective_id, has_side_effects=True, vmem_limit_bytes=LIMIT
    )


def cost(flops, nbytes):
    return pl.CostEstimate(flops=flops, bytes_accessed=nbytes, transcendentals=0)


def fast(inputs, tangent, token_ids, gate_weight, up_weight, down_weight, sketch, teacher_precision):
    model, hidden = gate_weight.shape
    feat, rank = sketch.shape
    coords = teacher_precision.shape[1]
    rows = token_ids.shape[0]
    fc = 1024
    nf = model // fc
    shape = jax.ShapeDtypeStruct

    depth = 32
    order = token_ids.reshape(NZ, NX, NC, 8).transpose(2, 1, 0, 3).reshape(rows)
    prec = pl.pallas_call(
        functools.partial(rows_kernel, depth),
        out_shape=shape((coords, rows), F32),
        in_specs=[pl.BlockSpec(memory_space=pltpu.SMEM), ANY],
        out_specs=IN_VMEM,
        scratch_shapes=[VMEM((depth, coords, 128), BF16), DMA((depth,))],
        name="precision_rows",
    )(order, teacher_precision.T)

    slots = 3
    xv = jnp.concatenate([inputs, tangent], axis=0)
    th, cg, ca, vc = pl.pallas_call(
        functools.partial(forward_kernel, nf, fc, slots, feat),
        out_shape=[
            shape((rows, hidden), BF16),
            shape((rows, hidden), F32),
            shape((rows, hidden), F32),
            shape((rows, feat), F32),
        ],
        in_specs=[IN_VMEM, ANY, ANY],
        out_specs=[IN_VMEM] * 4,
        scratch_shapes=[
            VMEM((2 * rows, model), BF16),
            VMEM((slots, fc, hidden), BF16),
            VMEM((slots, fc, hidden), BF16),
            VMEM((2 * rows, hidden), F32),
            VMEM((2 * rows, hidden), F32),
            DMA((2, slots)),
            DMA((nf, 3)), DMA((nf, 3)),
            DMA((nf,)), DMA((nf,)),
            DMA((nf,)), DMA((nf,)),
        ],
        compiler_params=params(0),
        cost_estimate=cost(8 * rows * model * hidden, 4 * model * hidden),
        name="gather_forward",
    )(xv, gate_weight, up_weight)

    width = model // NZ
    bg, bu, cot = pl.pallas_call(
        middle_kernel,
        out_shape=[shape((rows, hidden), BF16), shape((rows, hidden), BF16), shape((rows, feat), F32)],
        in_specs=[IN_VMEM] * 6 + [ANY],
        out_specs=[IN_VMEM] * 3,
        scratch_shapes=[
            VMEM((NZ, hidden, width), BF16),
            VMEM((NZ, rows, width), F32),
            VMEM((NZ, 2, rows, feat), F32),
            VMEM((NZ, rows, feat), BF16), VMEM((NZ, rows, feat), BF16),
            VMEM((3, rows, feat), BF16), VMEM((3, rows, feat), BF16),
            VMEM((NZ, NX, NC, coords, rows), F32),
            VMEM((NZ, NX, coords, rows), F32),
            VMEM((NZ, coords, rows), F32), VMEM((NZ, coords, rows), F32),
            VMEM((NZ, coords, rows), F32), VMEM((3, coords, rows), F32),
            VMEM((NZ, NX, NC, coords, rows), BF16),
            VMEM((NZ, NX, NC, rows, feat), BF16),
            VMEM((rows, hidden), F32),
            DMA((NZ,)),
            DMA((NZ, 4)), DMA((NZ, 4)),
            DMA((5,)), DMA((5,)),
            DMA((5,)), DMA((5,)),
            DMA((4, NZ)), DMA((4, NZ)),
        ],
        compiler_params=params(1),
        cost_estimate=cost(4 * rows * model * hidden, 2 * model * hidden),
        name="down_sketch_back",
    )(th, cg, ca, vc, sketch, prec, down_weight)

    return pl.pallas_call(
        functools.partial(final_kernel, nf, fc, slots),
        out_shape=shape((8, model), F32),
        in_specs=[IN_VMEM] * 3 + [ANY, ANY],
        out_specs=IN_VMEM,
        scratch_shapes=[
            VMEM((slots, fc, hidden), BF16),
            VMEM((slots, fc, hidden), BF16),
            VMEM((nf, rows, fc), F32),
            VMEM((nf, 64, fc), F32),
            VMEM((nf, 32, fc), BF16), VMEM((nf, 32, fc), BF16),
            VMEM((32, fc), F32),
            VMEM((nf, 3, 16, fc // 2), BF16), VMEM((nf, 3, 16, fc // 2), BF16),
            DMA((2, slots)),
            DMA((nf,)), DMA((nf,)),
            DMA((nf,)), DMA((nf,)),
            DMA((nf, 3)), DMA((nf, 3)),
        ],
        compiler_params=params(2),
        cost_estimate=cost(4 * rows * model * hidden, 4 * model * hidden),
        name="backward_scatter",
    )(bg, bu, cot, gate_weight, up_weight)


def general(inputs, tangent, token_ids, gate_weight, up_weight, down_weight, sketch, teacher_precision):
    rows_x, rows_v = (
        lax.all_gather(inputs, "tensor", axis=0, tiled=True),
        lax.all_gather(tangent, "tensor", axis=0, tiled=True),
    )
    position = lax.axis_index("tensor")
    feat_local = sketch.shape[0]
    offset = position * feat_local
    pre_gate = jnp.dot(rows_x, gate_weight, preferred_element_type=F32)
    pre_up = jnp.dot(rows_x, up_weight, preferred_element_type=F32)
    tan_gate = jnp.dot(rows_v, gate_weight, preferred_element_type=F32)
    tan_up = jnp.dot(rows_v, up_weight, preferred_element_type=F32)
    sig = jax.nn.sigmoid(pre_gate)
    act = pre_gate * sig
    slope = sig * (1.0 + pre_gate * (1.0 - sig))
    tan_hidden = (slope * tan_gate * pre_up + act * tan_up).astype(BF16)
    v_mine = lax.dynamic_slice_in_dim(rows_v, offset, feat_local, 1)
    own_term = jnp.dot(v_mine, sketch, preferred_element_type=F32)
    partial_value = jnp.dot(tan_hidden, down_weight, preferred_element_type=F32)
    summed_cols = lax.psum_scatter(partial_value, "tensor", scatter_dimension=1, tiled=True)
    sketch_part = (
        jnp.dot(summed_cols, sketch.astype(F32), precision=lax.Precision.HIGHEST) + own_term
    )
    sketch_cols = lax.psum_scatter(sketch_part, "tensor", scatter_dimension=1, tiled=True)
    rows_prec = teacher_precision[token_ids].astype(F32)
    weighted_cols = (rows_prec * sketch_cols).astype(BF16)
    weighted = lax.all_gather(weighted_cols, "tensor", axis=1, tiled=True)
    cot_cols = jnp.dot(weighted, sketch.T, preferred_element_type=F32)
    cot_full = lax.all_gather(cot_cols.astype(BF16), "tensor", axis=1, tiled=True)
    back_hidden = jnp.dot(cot_full, down_weight.T, preferred_element_type=F32)
    back_gate = (back_hidden * pre_up * slope).astype(BF16)
    back_up = (back_hidden * act).astype(BF16)
    result = jnp.dot(back_gate, gate_weight.T, preferred_element_type=F32)
    result = result + jnp.dot(back_up, up_weight.T, preferred_element_type=F32)
    current = lax.dynamic_slice_in_dim(result, offset, feat_local, 1)
    return lax.psum_scatter(
        lax.dynamic_update_slice_in_dim(result, current + cot_cols, offset, 1),
        "tensor",
        scatter_dimension=0,
        tiled=True,
    )


def solution(mesh):
    on_device = fast if mesh.shape["tensor"] == NZ * NX * NC else general
    return jax.shard_map(
        on_device,
        mesh=mesh,
        in_specs=(
            P(("groups", "tensor"), None),
            P(("groups", "tensor"), None),
            P("groups"),
            P(None, "tensor"),
            P(None, "tensor"),
            P("tensor", None),
            P("tensor", None),
            P(None, "tensor"),
        ),
        out_specs=P(("groups", "tensor"), None),
        check_vma=False,
    )
```

```python
import functools

import jax
import jax.numpy as jnp
from jax import lax
from jax.experimental import pallas as pl
from jax.experimental.pallas import tpu as pltpu
from jax.sharding import PartitionSpec as P

F32 = jnp.float32
BF16 = jnp.bfloat16
NZ, NX, NC = 4, 2, 2
MESH = pl.DeviceIdType.MESH
VMEM = pltpu.VMEM
DMA = pltpu.SemaphoreType.DMA
LIMIT = 62 << 20


def place():
    me = lax.axis_index("tensor")
    return me, me // 4, (me // 2) % 2, me % 2


def index_of(z, x, c):
    return (z % NZ) * 4 + x * 2 + c


def greet(z, x, c):
    barrier = pltpu.get_barrier_semaphore()
    others = [index_of(z + k, x, c) for k in (1, 2, 3)]
    others += [index_of(z, 1 - x, c), index_of(z, x, 1 - c)]
    for other in others:
        pl.semaphore_signal(barrier, inc=1, device_id={"tensor": other}, device_id_type=MESH)
    pl.semaphore_wait(barrier, 5)


def remote(src, dst, send, recv, other):
    return pltpu.make_async_remote_copy(
        src_ref=src,
        dst_ref=dst,
        send_sem=send,
        recv_sem=recv,
        device_id={"tensor": other},
        device_id_type=MESH,
    )


def span(start, size):
    return pl.ds(pl.multiple_of(start, size), size)


def loop(lo, hi, body):
    def step(i, carry):
        body(i)
        return carry

    lax.fori_loop(lo, hi, step, 0)


def nt(a, b):
    return lax.dot_general(a, b, (((1,), (1,)), ((), ())), preferred_element_type=F32)


def nn(a, b):
    return jnp.dot(a, b, preferred_element_type=F32)


def kernel(
    nf, fc, wc, slots, ahead, feat,
    in_ref, tan_ref, sk_ref, prec_ref, gate_ref, up_ref, down_ref, out_ref,
    xg, wg, wu, acc_g, acc_u, th, bu, vc, cot_own,
    dn, pbuf, rb, xsb, xrb, zsb, zrb, sk, rc, sxs, sxr, szs, szr, wga,
    bxs, bxr, bzs, bzr, tb,
    wsem, dsem, zs, zr, xs, xr, cs, cr,
    s_send, s_recv, k_send, k_recv, w_send, w_recv, a_send, a_recv,
    c_send, c_recv, x_send, x_recv, z_send, z_recv,
):
    me, z, x, c = place()
    x_peer, c_peer = index_of(z, 1 - x, c), index_of(z, x, 1 - c)
    hidden = th.shape[1]
    parts = fc // wc
    width = 4 * feat

    def weights(g):
        slot = lax.rem(g, slots)
        rows = span((g % (nf * parts)) * wc, wc)
        return (
            pltpu.make_async_copy(gate_ref.at[rows], wg.at[slot], wsem.at[0, slot]),
            pltpu.make_async_copy(up_ref.at[rows], wu.at[slot], wsem.at[1, slot]),
        )

    def fetch(g):
        for copy in weights(g):
            copy.start()

    def arrive(g):
        for copy in weights(g):
            copy.wait()

    def down(i):
        cols = span(((z + 1 + i) % NZ) * width, width)
        return pltpu.make_async_copy(down_ref.at[:, cols], dn.at[i], dsem.at[i])

    loop(0, slots, fetch)
    loop(0, NZ, lambda i: down(i).start())
    greet(z, x, c)


    slot_me = (c * NX + x) * NZ + z
    mine = span(slot_me * 16, 16)
    own = jnp.concatenate([in_ref[...].astype(F32), tan_ref[...].astype(F32)], axis=0)
    xg[mine, :] = own.astype(BF16)

    def gather_z(f, k):
        cols = span(f * fc, fc)
        return remote(
            xg.at[mine, cols], xg.at[mine, cols], zs.at[f, k - 1], zr.at[f, k - 1],
            index_of(z + k, x, c),
        )

    def gather_x(f, k):
        slot = (c * NX + x) * NZ + (z + NZ - k) % NZ
        part = xg.at[span(slot * 16, 16), span(f * fc, fc)]
        return remote(part, part, xs.at[f, k], xr.at[f, k], index_of(z, 1 - x, c))

    def gather_c(f):
        part = xg.at[span(c * 128, 128), span(f * fc, fc)]
        return remote(part, part, cs.at[f], cr.at[f], index_of(z, x, 1 - c))

    def first(f):
        for k in (1, 2, 3):
            gather_z(f, k).start()

    def first_x(f):
        gather_x(f, 0).start()

    first(0)
    first_x(0)
    loop(1, ahead, first)
    loop(1, nf, first_x)
    acc_g[...] = jnp.zeros_like(acc_g)
    acc_u[...] = jnp.zeros_like(acc_u)

    def forward_step(s):
        @pl.when(s < nf)
        def _():
            for k in (1, 2, 3):
                gather_z(s, k).wait_recv()
                gather_x(s, k).start()

            @pl.when(s + ahead < nf)
            def _():
                first(s + ahead)

        @pl.when((s >= 1) & (s <= nf))
        def _():
            for k in range(NZ):
                gather_x(s - 1, k).wait_recv()
            gather_c(s - 1).start()

        @pl.when(s >= 2)
        def _():
            f = s - 2
            gather_c(f).wait_recv()

            def piece(h):
                g = f * parts + h
                arrive(g)
                slot = lax.rem(g, slots)
                block = xg[:, span(g * wc, wc)]
                acc_g[...] += nn(block, wg[slot])
                acc_u[...] += nn(block, wu[slot])
                fetch(g + slots)

            loop(0, parts, piece)

    loop(0, nf + 2, forward_step)

    tile = 256

    def finish(t):
        cols = span(t * tile, tile)
        both_g = acc_g[:, cols].reshape(16, 2, 8, tile)
        both_u = acc_u[:, cols].reshape(16, 2, 8, tile)
        pre_gate, tan_gate = both_g[:, 0].reshape(128, tile), both_g[:, 1].reshape(128, tile)
        pre_up, tan_up = both_u[:, 0].reshape(128, tile), both_u[:, 1].reshape(128, tile)
        sig = jax.nn.sigmoid(pre_gate)
        act = pre_gate * sig
        slope = sig * (1.0 + pre_gate * (1.0 - sig))
        coef = pre_up * slope
        th[:, cols] = (slope * tan_gate * pre_up + act * tan_up).astype(BF16)
        acc_g[0:128, cols] = coef
        acc_u[0:128, cols] = act

    loop(0, hidden // tile, finish)
    own = xg[:, span(me * feat, feat)].astype(F32).reshape(16, 2, 8, feat)
    vc[...] = own[:, 1].reshape(128, feat)

    def forward_drain(f):
        for k in (1, 2, 3):
            gather_z(f, k).wait_send()
        for k in range(NZ):
            gather_x(f, k).wait_send()
        gather_c(f).wait_send()

    loop(0, nf, forward_drain)


    def cols_of(xx, cc):
        return span((xx * 2 + cc) * feat, feat)

    def features(k, xx, cc):
        return span(index_of(z + NZ - k, xx, cc) * feat, feat)

    def rs_c(i, xx):
        return remote(
            pbuf.at[i * 2 + xx, :, span((1 - c) * feat, feat)], rb.at[i, :, span(xx * feat, feat)],
            s_send.at[i, xx], s_recv.at[i, xx], c_peer,
        )

    def rs_x(i):
        return remote(xsb.at[i], xrb.at[i], s_send.at[i, 2], s_recv.at[i, 2], x_peer)

    def rs_z(i):
        return remote(
            zsb.at[i], zrb.at[i], s_send.at[i, 3], s_recv.at[i, 3], index_of(z + 1 + i, x, c)
        )

    def summed_c(i, xx):
        return pbuf[i * 2 + xx, :, span(c * feat, feat)] + rb[i, :, span(xx * feat, feat)]

    def middle_step(s):
        @pl.when(s < NZ)
        def _():
            down(s).wait()

            def tile(t):
                cols = span(t * feat, feat)
                held = nn(th[...], dn[s, :, cols])
                pbuf[s * 2 + t // 2, :, span((t % 2) * feat, feat)] = held

            loop(0, 4, tile)
            rs_c(s, 0).start()
            rs_c(s, 1).start()

        @pl.when((s >= 1) & (s <= NZ))
        def _():
            i = s - 1
            rs_c(i, 0).wait_recv()
            rs_c(i, 1).wait_recv()
            xsb[i] = (summed_c(i, 1 - x)).astype(BF16)
            rs_x(i).start()

        @pl.when((s >= 2) & (s <= NZ))
        def _():
            i = s - 2
            rs_x(i).wait_recv()
            total = summed_c(i, x) + xrb[i].astype(F32)
            zsb[i] = total.astype(BF16)
            rs_z(i).start()

    loop(0, NZ + 1, middle_step)
    last = NZ - 1
    rs_x(last).wait_recv()
    total = summed_c(last, x) + xrb[last].astype(F32) + vc[...]
    for i in range(NZ - 1):
        rs_z(i).wait_recv()
        total = total + zrb[i].astype(F32)

    high = total.astype(BF16)
    low = (total - high.astype(F32)).astype(BF16)
    part = nn(high, sk_ref[...]) + nn(low, sk_ref[...])
    sk[...] = part.T.reshape(sk.shape)
    copy_c = remote(sk.at[:, :, 1 - c], rc, k_send.at[0], k_recv.at[0], c_peer)
    copy_c.start()
    copy_c.wait_recv()
    sxs[...] = sk[:, 1 - x, c] + rc[:, 1 - x]
    copy_x = remote(sxs, sxr, k_send.at[1], k_recv.at[1], x_peer)
    copy_x.start()
    copy_x.wait_recv()
    szs[...] = sk[:, x, c] + rc[:, x] + sxr[...]
    copies = [
        remote(szs.at[(z + k) % NZ], szr.at[k - 1], k_send.at[1 + k], k_recv.at[1 + k],
               index_of(z + k, x, c))
        for k in (1, 2, 3)
    ]
    for copy in copies:
        copy.start()
    value = szs[z]
    for k, copy in enumerate(copies):
        copy.wait_recv()
        value = value + szr[k]
    for copy in copies + [copy_c, copy_x]:
        copy.wait_send()

    wga[z, x, c] = (prec_ref[...] * value).astype(BF16)
    mine = wga.at[z, x, c]
    copies = [
        remote(mine, mine, w_send.at[k - 1], w_recv.at[k - 1], index_of(z + k, x, c))
        for k in (1, 2, 3)
    ]
    for copy in copies:
        copy.start()
    for copy in copies:
        copy.wait_recv()
    copy_x = remote(wga.at[:, x, c], wga.at[:, x, c], w_send.at[3], w_recv.at[3], x_peer)
    copy_x.start()
    copy_x.wait_recv()
    copy_c = remote(wga.at[:, :, c], wga.at[:, :, c], w_send.at[4], w_recv.at[4], c_peer)
    copy_c.start()
    copy_c.wait_recv()
    for copy in copies + [copy_x, copy_c]:
        copy.wait_send()
    flat = wga[...].reshape(-1, 128).astype(F32).T.astype(BF16)
    cot = nt(flat, sk_ref[...])
    cot_own[...] = cot

    xg[0:128, features(0, x, c)] = cot.astype(BF16)

    half = 64

    def ag_z(h, k):
        part = xg.at[pl.ds(h * half, half), features(0, x, c)]
        return remote(part, part, a_send.at[h, k], a_recv.at[h, k], index_of(z + k, x, c))

    def ag_x(h, k):
        part = xg.at[pl.ds(h * half, half), features(k, x, c)]
        return remote(part, part, a_send.at[2 + h, k], a_recv.at[2 + h, k], x_peer)

    def ag_c(k, own):
        part = xg.at[pl.ds(0, 128), features(k, x if own else 1 - x, c)]
        row = 4 if own else 5
        return remote(part, part, a_send.at[row, k], a_recv.at[row, k], c_peer)

    def use(k, xx, cc):
        acc_g[128:256, :] += nt(xg[0:128, features(k, xx, cc)], dn[3 - k, :, cols_of(xx, cc)])

    for h in (0, 1):
        for k in (1, 2, 3):
            ag_z(h, k).start()
        ag_x(h, 0).start()
    ag_c(0, True).start()
    acc_g[128:256, :] = jnp.zeros((128, acc_g.shape[1]), F32)
    use(0, x, c)
    for h in (0, 1):
        for k in (1, 2, 3):
            ag_z(h, k).wait_recv()
            ag_x(h, k).start()
            if h:
                ag_c(k, True).start()

    def own_column(k):
        use(k, x, c)

    loop(1, NZ, own_column)

    def pass_on(k):
        ag_x(0, k).wait_recv()
        ag_x(1, k).wait_recv()
        ag_c(k, False).start()

    loop(0, NZ, pass_on)

    def sibling_own(k):
        ag_c(k, True).wait_recv()
        use(k, x, 1 - c)

    loop(0, NZ, sibling_own)

    def other_column(k):
        use(k, 1 - x, c)

    loop(0, NZ, other_column)

    def sibling_other(k):
        ag_c(k, False).wait_recv()
        use(k, 1 - x, 1 - c)

    loop(0, NZ, sibling_other)

    th[...] = (acc_g[128:256, :] * acc_g[0:128, :]).astype(BF16)
    bu[...] = (acc_g[128:256, :] * acc_u[0:128, :]).astype(BF16)

    def middle_drain(k):
        @pl.when(k >= 1)
        def _():
            ag_z(0, k).wait_send()
            ag_z(1, k).wait_send()
            rs_z(k - 1).wait_send()

        ag_x(0, k).wait_send()
        ag_x(1, k).wait_send()
        ag_c(k, True).wait_send()
        ag_c(k, False).wait_send()
        rs_c(k, 0).wait_send()
        rs_c(k, 1).wait_send()
        rs_x(k).wait_send()

    loop(0, NZ, middle_drain)

    half_c = fc // 2

    def back_c(f):
        return remote(
            pbuf.at[f, span((1 - c) * 64, 64)], rb.at[f // 2, span((f % 2) * 64, 64)], c_send.at[f], c_recv.at[f], c_peer
        )

    def back_x(f):
        return remote(bxs.at[f], bxr.at[f], x_send.at[f], x_recv.at[f], x_peer)

    def back_z(f, k):
        return remote(
            bzs.at[f, k - 1], bzr.at[f, k - 1], z_send.at[f, k - 1], z_recv.at[f, k - 1],
            index_of(z + k, x, c),
        )

    def final_step(s):
        @pl.when(s < nf)
        def _():

            def piece(h):
                g = (nf + s) * parts + h
                arrive(g)
                slot = lax.rem(g, slots)
                pbuf[s, :, span(h * wc, wc)] = nt(th[...], wg[slot]) + nt(bu[...], wu[slot])

                @pl.when(g + slots < 2 * nf * parts)
                def _():
                    fetch(g + slots)

            loop(0, parts, piece)

            @pl.when(s == (me * feat) // fc)
            def _():
                cols = span(((me * feat) % fc) // feat * feat, feat)
                pbuf[s, :, cols] += cot_own[...]

            back_c(s).start()

        @pl.when((s >= 1) & (s <= nf))
        def _():
            f = s - 1
            back_c(f).wait_recv()
            away = pbuf[f, span(c * 64 + (1 - x) * 32, 32)] + rb[f // 2, span((f % 2) * 64 + (1 - x) * 32, 32)]
            bxs[f] = away.astype(BF16)
            back_x(f).start()

        @pl.when((s >= 2) & (s <= nf + 1))
        def _():
            f = s - 2
            back_x(f).wait_recv()
            tb[...] = (
                pbuf[f, span(c * 64 + x * 32, 32)]
                + rb[f // 2, span((f % 2) * 64 + x * 32, 32)]
                + bxr[f].astype(F32)
            )
            for k in (1, 2, 3):
                rows = tb[span(((z + k) % NZ) * 8, 8), :]
                folded = jnp.concatenate([rows[:, :half_c], rows[:, half_c:]], axis=0)
                bzs[f, k - 1] = folded.astype(BF16)
                back_z(f, k).start()
            out_ref[:, span(f * fc, fc)] = tb[span(z * 8, 8), :]

        @pl.when(s >= 3)
        def _():
            f = s - 3
            total = out_ref[:, span(f * fc, fc)]
            for k in (1, 2, 3):
                back_z(f, k).wait_recv()
                folded = bzr[f, k - 1].astype(F32)
                total = total + jnp.concatenate([folded[:8], folded[8:]], axis=1)
            out_ref[:, span(f * fc, fc)] = total

    loop(0, nf + 3, final_step)

    def final_drain(f):
        back_c(f).wait_send()
        back_x(f).wait_send()
        for k in (1, 2, 3):
            back_z(f, k).wait_send()

    loop(0, nf, final_drain)


def rows_kernel(ids_ref, table_ref, out_ref, buf, sem):
    count = out_ref.shape[1]
    unroll = 8

    def token(t):
        block = ((t // 8) % NZ) * 4 + ((t // 32) % NX) * 2 + t // 64
        return ids_ref[block * 8 + t % 8]

    def copy(t):
        block = pl.multiple_of(lax.shift_right_logical(token(t), 7) * 128, 128)
        return pltpu.make_async_copy(table_ref.at[:, pl.ds(block, 128)], buf.at[t], sem.at[t])

    def start(g):
        for r in range(unroll):
            copy(g * unroll + r).start()

    loop(0, count // unroll, start)
    lanes = lax.broadcasted_iota(jnp.int32, out_ref.shape, 1)

    def step(g, held):
        first = g * unroll
        for r in range(unroll):
            copy(first + r).wait()
        for r in range(unroll):
            t = first + r
            block = buf[t].astype(F32)
            shift = jnp.bitwise_and(t + 128 - jnp.bitwise_and(token(t), 127), 127)
            held = jnp.where(lanes == t, pltpu.roll(block, shift, axis=1), held)
        return held

    out_ref[...] = lax.fori_loop(0, count // unroll, step, jnp.zeros(out_ref.shape, F32))


ANY = pl.BlockSpec(memory_space=pl.ANY)
IN_VMEM = pl.BlockSpec(memory_space=pltpu.VMEM)


def params(collective_id):
    return pltpu.CompilerParams(
        collective_id=collective_id, has_side_effects=True, vmem_limit_bytes=LIMIT
    )


def cost(flops, nbytes):
    return pl.CostEstimate(flops=flops, bytes_accessed=nbytes, transcendentals=0)


def fast(inputs, tangent, token_ids, gate_weight, up_weight, down_weight, sketch, teacher_precision):
    model, hidden = gate_weight.shape
    feat, rank = sketch.shape
    coords = teacher_precision.shape[1]
    rows = token_ids.shape[0]
    fc = 1024
    nf = model // fc
    shape = jax.ShapeDtypeStruct

    prec = pl.pallas_call(
        rows_kernel,
        out_shape=shape((coords, rows), F32),
        in_specs=[pl.BlockSpec(memory_space=pltpu.SMEM), ANY],
        out_specs=IN_VMEM,
        scratch_shapes=[VMEM((rows, coords, 128), BF16), DMA((rows,))],
        name="precision_rows",
    )(token_ids, teacher_precision.T)

    slots = 2
    wc = fc // 2
    width = model // NZ
    return pl.pallas_call(
        functools.partial(kernel, nf, fc, wc, slots, min(3, nf), feat),
        out_shape=shape((8, model), F32),
        in_specs=[IN_VMEM] * 4 + [ANY] * 3,
        out_specs=IN_VMEM,
        scratch_shapes=[
            VMEM((2 * rows, model), BF16),
            VMEM((slots, wc, hidden), BF16),
            VMEM((slots, wc, hidden), BF16),
            VMEM((2 * rows, hidden), F32),
            VMEM((2 * rows, hidden), F32),
            VMEM((rows, hidden), BF16), VMEM((rows, hidden), BF16),
            VMEM((rows, feat), F32), VMEM((rows, feat), F32),
            VMEM((NZ, hidden, width), BF16),
            VMEM((nf, rows, fc), F32),
            VMEM((NZ, rows, 2 * feat), F32),
            VMEM((NZ, rows, feat), BF16), VMEM((NZ, rows, feat), BF16),
            VMEM((3, rows, feat), BF16), VMEM((3, rows, feat), BF16),
            VMEM((NZ, NX, NC, coords, rows), F32),
            VMEM((NZ, NX, coords, rows), F32),
            VMEM((NZ, coords, rows), F32), VMEM((NZ, coords, rows), F32),
            VMEM((NZ, coords, rows), F32), VMEM((3, coords, rows), F32),
            VMEM((NZ, NX, NC, coords, rows), BF16),
            VMEM((nf, 32, fc), BF16), VMEM((nf, 32, fc), BF16),
            VMEM((nf, 3, 16, fc // 2), BF16), VMEM((nf, 3, 16, fc // 2), BF16),
            VMEM((32, fc), F32),
            DMA((2, slots)), DMA((NZ,)),
            DMA((nf, 3)), DMA((nf, 3)),
            DMA((nf, NZ)), DMA((nf, NZ)),
            DMA((nf,)), DMA((nf,)),
            DMA((NZ, 4)), DMA((NZ, 4)),
            DMA((5,)), DMA((5,)),
            DMA((5,)), DMA((5,)),
            DMA((6, NZ)), DMA((6, NZ)),
            DMA((nf,)), DMA((nf,)),
            DMA((nf,)), DMA((nf,)),
            DMA((nf, 3)), DMA((nf, 3)),
        ],
        compiler_params=params(0),
        cost_estimate=cost(16 * rows * model * hidden, 10 * model * hidden),
        name="gauss_newton",
    )(inputs, tangent, sketch, prec, gate_weight, up_weight, down_weight)


def general(inputs, tangent, token_ids, gate_weight, up_weight, down_weight, sketch, teacher_precision):
    rows_x, rows_v = (
        lax.all_gather(inputs, "tensor", axis=0, tiled=True),
        lax.all_gather(tangent, "tensor", axis=0, tiled=True),
    )
    position = lax.axis_index("tensor")
    feat_local = sketch.shape[0]
    offset = position * feat_local
    pre_gate = jnp.dot(rows_x, gate_weight, preferred_element_type=F32)
    pre_up = jnp.dot(rows_x, up_weight, preferred_element_type=F32)
    tan_gate = jnp.dot(rows_v, gate_weight, preferred_element_type=F32)
    tan_up = jnp.dot(rows_v, up_weight, preferred_element_type=F32)
    sig = jax.nn.sigmoid(pre_gate)
    act = pre_gate * sig
    slope = sig * (1.0 + pre_gate * (1.0 - sig))
    tan_hidden = (slope * tan_gate * pre_up + act * tan_up).astype(BF16)
    v_mine = lax.dynamic_slice_in_dim(rows_v, offset, feat_local, 1)
    own_term = jnp.dot(v_mine, sketch, preferred_element_type=F32)
    partial_value = jnp.dot(tan_hidden, down_weight, preferred_element_type=F32)
    summed_cols = lax.psum_scatter(partial_value, "tensor", scatter_dimension=1, tiled=True)
    sketch_part = (
        jnp.dot(summed_cols, sketch.astype(F32), precision=lax.Precision.HIGHEST) + own_term
    )
    sketch_cols = lax.psum_scatter(sketch_part, "tensor", scatter_dimension=1, tiled=True)
    rows_prec = teacher_precision[token_ids].astype(F32)
    weighted_cols = (rows_prec * sketch_cols).astype(BF16)
    weighted = lax.all_gather(weighted_cols, "tensor", axis=1, tiled=True)
    cot_cols = jnp.dot(weighted, sketch.T, preferred_element_type=F32)
    cot_full = lax.all_gather(cot_cols.astype(BF16), "tensor", axis=1, tiled=True)
    back_hidden = jnp.dot(cot_full, down_weight.T, preferred_element_type=F32)
    back_gate = (back_hidden * pre_up * slope).astype(BF16)
    back_up = (back_hidden * act).astype(BF16)
    result = jnp.dot(back_gate, gate_weight.T, preferred_element_type=F32)
    result = result + jnp.dot(back_up, up_weight.T, preferred_element_type=F32)
    current = lax.dynamic_slice_in_dim(result, offset, feat_local, 1)
    return lax.psum_scatter(
        lax.dynamic_update_slice_in_dim(result, current + cot_cols, offset, 1),
        "tensor",
        scatter_dimension=0,
        tiled=True,
    )


def solution(mesh):
    on_device = fast if mesh.shape["tensor"] == NZ * NX * NC else general
    return jax.shard_map(
        on_device,
        mesh=mesh,
        in_specs=(
            P(("groups", "tensor"), None),
            P(("groups", "tensor"), None),
            P("groups"),
            P(None, "tensor"),
            P(None, "tensor"),
            P("tensor", None),
            P("tensor", None),
            P(None, "tensor"),
        ),
        out_specs=P(("groups", "tensor"), None),
        check_vma=False,
    )
```
